32 devices in a mesh: row: 4 (over z), col: 8 (over y, x, core).
Axes of the slice: x: 2, y: 2, z: 4, core: 2. Of those that a mesh axis runs over, the one named last changes fastest.
Arguments:
- vectors: float32 [1536, 48, 128], P('row', 'col'), may hold values from -0.078125 to 0.078125
- hblocks: float32 [48, 7, 128, 128], P('col'), may hold values from -1 to 1, as said below
- coupling: int32 [48, 6], P('col'), may hold values from 0 to 1, as said below
Outputs:
- projected_ham: float32 [1536, 1536], P('row', 'col')
- intersection: float32 [1536, 1536], P('row', 'col')
The draws below stay inside these ranges and needn't reach their ends.
Inputs may be any that keep to these rules, and one draw needn't show every extreme that they name: For 1 <= k <= 3 and a >= k, hblocks[a, 3 - k] is the transpose of hblocks[a - k, 3 + k], and hblocks[a, 3] is symmetric, so the Hamiltonian is symmetric. coupling[a, 3 + k - 1] equals coupling[a + k, 3 - k] for 1 <= k <= 3; entries that name an atom outside the chain are 0.
All inputs are finite; a program needn't handle non-finite values.
Results may differ from the reference program's by a relative error of at most 0.0001.
Values sent between devices are 32-bit elements; how exact they have to be, the bound alone decides.
No kernel may reach another device: no remote copies, remote signals or barrier semaphores. Data moves between devices by JAX's collectives and lax.ppermute only.
A program may use at most 64 MiB of HBM per device.

```python
import jax
import jax.numpy as jnp
from jax import lax

BLOCK = 128
STATES = 1536
REACH = 3
DEGREE = 3
ATOMS = 48
BASIS = 6144


def draw_hblocks(key, part):
    key = jax.random.fold_in(key, 11)
    shape = (ATOMS, REACH + 1, BLOCK, BLOCK)
    raw = jnp.clip(0.3 * jax.random.normal(key, shape, jnp.float32), -1.0, 1.0)
    middle = 0.5 * (raw[:, 0] + jnp.swapaxes(raw[:, 0], -1, -2))
    lefts = []
    rights = []
    for offset in range(1, REACH + 1):
        rights.append(raw[:, offset])
        lefts.append(jnp.swapaxes(jnp.roll(raw[:, offset], offset, axis=0), -1, -2))
    ordered = lefts[::-1] + [middle] + rights
    return jnp.stack(ordered, axis=1)


def draw_coupling(key, part):
    key = jax.random.fold_in(key, 23)
    bonds = (jax.random.randint(key, (ATOMS, REACH), 0, 4) > 0).astype(jnp.int32)
    places = jnp.arange(ATOMS, dtype=jnp.int32)[:, None]
    reach_ids = jnp.arange(1, REACH + 1, dtype=jnp.int32)[None, :]
    bonds = bonds * (places + reach_ids < ATOMS).astype(jnp.int32)
    lefts = []
    for offset in range(1, REACH + 1):
        lefts.append(jnp.roll(bonds[:, offset - 1], offset, axis=0))
    left_part = jnp.stack(lefts[::-1], axis=1)
    return jnp.concatenate([left_part, bonds], axis=1)


def shard_levels(rng, dims, split, low, largest):
    level = 1.0
    for axis_at, parts in split:
        draws = jax.random.uniform(jax.random.fold_in(jax.random.fold_in(rng, 6), axis_at), (parts,), jnp.float32, low / len(split), largest / len(split))
        level = level * jnp.repeat(jnp.exp(draws), dims[axis_at] // parts).reshape((-1,) + (1,) * (len(dims) - 1 - axis_at))
    return level


def gaussian(own_key, extent, deviation, limit, shards=(), held_as=jnp.bfloat16):
    array = jax.random.normal(own_key, extent, jnp.float32) * deviation
    if len(shards) > 0:
        array = shard_levels(own_key, extent, shards, -0.22, 0.18) * array
    return jnp.clip(array, min=-limit, max=limit).astype(held_as)


def setup_inputs(seed: int = 0) -> dict:
    streams_of = jax.random.split(jax.random.key(seed), 4)
    return {
        "vectors": gaussian(streams_of[0], (STATES, ATOMS, BLOCK), BASIS ** -0.5, 0.078125, ((0, 4), (1, 8)), jnp.float32),
        "hblocks": draw_hblocks(jax.random.fold_in(streams_of[3], 71), 0),
        "coupling": draw_coupling(jax.random.fold_in(streams_of[3], 71), 0),
    }


CENTER = 0.5
HALF_WIDTH = 1.5
HSCALE = 0.1


def masked_blocks(hblocks, coupling):
    ones = jnp.ones((coupling.shape[0], 1), jnp.int32)
    presence = jnp.concatenate([coupling[:, :REACH], ones, coupling[:, REACH:]], axis=1)
    return HSCALE * hblocks * presence.astype(jnp.float32)[:, :, None, None]


def apply_ham(field, blocks):
    atoms = field.shape[1]
    padded = jnp.pad(field, ((0, 0), (REACH, REACH), (0, 0)))
    result = jnp.zeros(field.shape, jnp.float32)
    for offset in range(2 * REACH + 1):
        shifted = padded[:, offset:offset + atoms, :]
        result = result + jnp.einsum("saj,aij->sai", shifted, blocks[:, offset], precision=lax.Precision.HIGHEST)
    return result


def reference(vectors, hblocks, coupling):
    blocks = masked_blocks(hblocks, coupling)
    y_prev = vectors
    y_now = (apply_ham(vectors, blocks) - CENTER * vectors) / HALF_WIDTH
    for section in range(DEGREE - 1):
        y_next = 2.0 * (apply_ham(y_now, blocks) - CENTER * y_now) / HALF_WIDTH - y_prev
        y_prev = y_now
        y_now = y_next
    image = apply_ham(y_now, blocks)
    flat_y = y_now.reshape(y_now.shape[0], -1)
    flat_w = image.reshape(image.shape[0], -1)
    projected_ham = jnp.einsum("sn,tn->st", flat_y, flat_w, precision=lax.Precision.HIGHEST)
    intersection = jnp.einsum("sn,tn->st", flat_y, flat_y, precision=lax.Precision.HIGHEST)
    return (projected_ham, intersection)
```

```python
import functools

import jax
import jax.numpy as jnp
from jax import lax
from jax.experimental import pallas as pl
from jax.experimental.pallas import tpu as pltpu
from jax.sharding import PartitionSpec as P

REACH = 3
DEGREE = 3
CENTER = 0.5
HALF_WIDTH = 1.5
HSCALE = 0.1
PARTS = 2

WHOLE = pl.BlockSpec(memory_space=pltpu.VMEM)
SCALARS = pl.BlockSpec(memory_space=pltpu.SMEM)
ANYWHERE = pl.BlockSpec(memory_space=pl.ANY)
NN = ((1,), (0,))


def call(kernel, out_shape, arrays, specs, name, mib, flops=0, scratch=(), after=()):
    outs = list(out_shape)
    moved = sum(a.size * a.dtype.itemsize for a in list(arrays) + outs)
    count, made, late = len(arrays), len(outs), len(after)

    def body(*refs):
        inner = refs[count + late :]
        kernel(*refs[:count], *inner[:made], *inner[made + late :])

    return list(pl.pallas_call(
        body,
        out_shape=outs + [jax.ShapeDtypeStruct(a.shape, a.dtype) for a in after],
        in_specs=[*specs] + [ANYWHERE] * late,
        out_specs=[WHOLE] * made + [ANYWHERE] * late,
        scratch_shapes=list(scratch),
        input_output_aliases={count + i: made + i for i in range(late)},
        compiler_params=pltpu.CompilerParams(vmem_limit_bytes=mib * 1024 * 1024),
        cost_estimate=pl.CostEstimate(flops=int(flops), bytes_accessed=moved, transcendentals=0),
        name=name,
    )(*arrays, *after))


def f32(*shape):
    return jax.ShapeDtypeStruct(shape, jnp.float32)


def bf16(*shape):
    return jax.ShapeDtypeStruct(shape, jnp.bfloat16)


def split(x):
    high = x.astype(jnp.bfloat16)
    low = (x - high.astype(jnp.float32)).astype(jnp.bfloat16)
    return high, low


def dot(a, b):
    return lax.dot_general(a, b, (NN, ((), ())), preferred_element_type=jnp.float32)


def dot3(a, b):
    rows = a[0].shape[0]
    both = dot(jnp.concatenate(a, axis=0), b[0])
    return both[:rows] + (both[rows:] + dot(a[0], b[1]))


def arrange_kernel(groups, width, odd_ref, v_ref, mine_ref, theirs_ref, *parts):
    odd = odd_ref[0]
    atoms, states, size = v_ref.shape
    half = atoms // 2
    rows = states // PARTS
    for k in range(atoms):
        column = v_ref[jnp.where(odd == 1, atoms - 1 - k, k)]
        at = slice((k % half) * size, (k % half + 1) * size)
        for part in range(PARTS):
            parts[2 * part + k // half][:, at] = column[part * rows : (part + 1) * rows]
        for group in range(groups):
            low = column[2 * group * width : (2 * group + 1) * width]
            high = column[(2 * group + 1) * width : (2 * group + 2) * width]
            to = slice(group * width, (group + 1) * width)
            mine_ref[to, k * size : (k + 1) * size] = jnp.where(odd == 1, high, low)
            theirs_ref[to, k * size : (k + 1) * size] = jnp.where(odd == 1, low, high)


def arrange(odd, vectors, width):
    states, atoms, size = vectors.shape
    out = [f32(states // 2, atoms * size)] * 2 + [f32(states // PARTS, atoms // 2 * size)] * (2 * PARTS)
    kernel = functools.partial(arrange_kernel, states // (2 * width), width)
    by_atom = jnp.transpose(vectors, (1, 0, 2))
    mine, theirs, *parts = call(kernel, out, [odd, by_atom], [SCALARS, WHOLE], "arrange", 8)
    return mine, theirs, [parts[2 * p : 2 * p + 2] for p in range(PARTS)]


def weights_kernel(atoms, odd_ref, coupling_ref, h_ref, own_h, own_l, far_h, far_l, near_h, near_l):
    odd = odd_ref[0]
    size = h_ref.shape[-1]

    def block(k, d):
        a = jnp.where(odd == 1, atoms - 1 - k, k)
        s = jnp.where(odd == 1, -d, d)
        h = HSCALE * h_ref[a, s + REACH]
        if d != 0:
            place = jnp.where(s < 0, s + REACH, s + REACH - 1)
            h = h * coupling_ref[a, place].astype(jnp.float32)
        return split(h.T)

    def put(high_ref, low_ref, row, column, value):
        rows = slice(row * size, (row + 1) * size)
        columns = slice(column * size, (column + 1) * size)
        high_ref[rows, columns], low_ref[rows, columns] = value

    zero = jnp.zeros((size, size), jnp.bfloat16)
    for m in range(atoms):
        for k in range(atoms):
            put(own_h, own_l, m, k, block(k, m - k) if abs(m - k) <= REACH else (zero, zero))
    for n in range(REACH):
        for j in range(REACH):
            d = -1 - n - j
            put(far_h, far_l, n, j, block(j, d) if d >= -REACH else (zero, zero))
            k = atoms - REACH + j
            d = atoms + REACH - 1 - n - k
            put(near_h, near_l, n, j, block(k, d) if d <= REACH else (zero, zero))


def make_weights(odd, coupling, hblocks):
    atoms, size = hblocks.shape[0], hblocks.shape[-1]
    full, edge = atoms * size, REACH * size
    out = [bf16(full, full)] * 2 + [bf16(edge, edge)] * 4
    kernel = functools.partial(weights_kernel, atoms)
    return call(kernel, out, [odd, coupling, hblocks], [SCALARS, SCALARS, WHOLE], "weights", 10)


def base_kernel(scales, high_ref, low_ref, *rest):
    out_ref = rest[-1]
    fields = [(rest[2 * i], rest[2 * i + 1]) for i in range((len(rest) - 1) // 2)]
    edge = rest[0].shape[1]
    halves = [split(ref[...]) for ref in fields[0]]
    operand = [jnp.concatenate([halves[0][term], halves[1][term]], axis=1) for term in range(2)]
    for side in range(2):
        columns = slice(side * edge, (side + 1) * edge)
        value = scales[0] * dot3(operand, (high_ref[:, columns], low_ref[:, columns]))
        for scale, field in zip(scales[1:], fields):
            if scale:
                value = value + scale * field[side][...]
        out_ref[:, columns] = value


def make_base(scales, weights, fields, after):
    arrays = list(weights[:2]) + [half for field in fields for half in field]
    rows, edge = fields[0][0].shape
    flops = 6 * rows * 4 * edge * edge
    return call(functools.partial(base_kernel, scales), [f32(rows, 2 * edge)], arrays, [WHOLE] * len(arrays), "base", 10, flops, (), after)


def tail_kernel(scale, base, got_far, got_near, fh, fl, nh, nl, *outs):
    edge = got_far.shape[1]
    for side, (got, high, low) in enumerate(((got_far, fh, fl), (got_near, nh, nl))):
        columns = slice(side * edge, (side + 1) * edge)
        value = base[:, columns] + scale * dot3(split(got[...]), (high[...], low[...]))
        if len(outs) == 2:
            outs[side][...] = value
        else:
            outs[0][:, columns] = value


def make_tail(scale, base, got, weights, joined, after):
    arrays = [base, *got, *weights[2:]]
    rows, edge = got[0].shape
    out = [f32(rows, 2 * edge)] if joined else [f32(rows, edge)] * 2
    flops = 6 * rows * 2 * edge * edge
    return call(functools.partial(tail_kernel, scale), out, arrays, [WHOLE] * len(arrays), "tail", 8, flops, (), after)


def assemble_kernel(all_ref, *outs):
    planes, _, rows, depth = all_ref.shape
    step = 128
    for side in range(2):
        for at in range(0, depth, step):
            columns = [all_ref[plane, side, :, at : at + step] for plane in range(planes)]
            term = split(jnp.concatenate(columns, axis=0).T)
            outs[2 * side][at : at + step], outs[2 * side + 1][at : at + step] = term


def assemble(gathered, after):
    planes, _, rows, depth = gathered.shape
    out = [bf16(depth, planes * rows)] * 4
    return call(assemble_kernel, out, [gathered], [WHOLE], "assemble", 10, 0, (), after)


def product_kernel(own_h, own_l, other_h, other_l, *rest):
    out_ref = rest[-1]
    half = len(rest) // 2
    value = dot3(split(joined(rest[:half])), (own_h[...], own_l[...]))
    value = value + dot3(split(joined(rest[half:-1])), (other_h[...], other_l[...]))
    out_ref[...] = value.T


def joined(refs):
    parts = len(refs) // PARTS
    rows = [
        jnp.concatenate([ref[...] for ref in refs[parts * p : parts * (p + 1)]], axis=1) for p in range(PARTS)
    ]
    return jnp.concatenate(rows, axis=0)


def product(everything, own, other):
    depth, width = everything[0].shape
    arrays = [*everything] + [half for part in own + other for half in part]
    rows = sum(part[0].shape[0] for part in own)
    flops = 12 * rows * depth * width
    return call(product_kernel, [f32(width, rows)], arrays, [WHOLE] * len(arrays), "product", 14, flops)[0]


def halve(part, axis_at, mine, count, bit):
    other = lax.dynamic_index_in_dim(part, 1 - mine, axis_at, keepdims=False)
    kept = lax.dynamic_index_in_dim(part, mine, axis_at, keepdims=False)
    return kept + lax.ppermute(other, "col", [(i, i ^ (1 << bit)) for i in range(count)])


def reduce_step(part, step, low_first):
    count = lax.axis_size("col")
    me = lax.axis_index("col").astype(jnp.int32)
    bits = count.bit_length() - 1
    if step == 1:
        part = part.reshape((2,) * (bits - 1) + (part.shape[0] * 2 // count, part.shape[1]))
    bit = step if low_first else bits - step
    return halve(part, bits - 1 - step if low_first else 0, (me >> bit) % 2, count, bit)


def reduce_rest(part, done, low_first):
    bits = lax.axis_size("col").bit_length() - 1
    for step in range(done + 1, bits):
        part = reduce_step(part, step, low_first)
    return part


def per_device(vectors, hblocks, coupling):
    count = lax.axis_size("col")
    me = lax.axis_index("col").astype(jnp.int32)
    odd = (me % 2).reshape(1)
    width = vectors.shape[0] * lax.axis_size("row") // count
    inner = [(i, i ^ 1) for i in range(count)]
    outer = [(i, i + 1) for i in range(1, count - 1, 2)]
    outer = outer + [(b, a) for a, b in outer]

    mine, theirs, start = arrange(odd, vectors, width)
    weights = make_weights(odd, coupling, hblocks)
    groups = mine.shape[0] // width
    cut = width // 24 * 16 or width
    payload = [x.reshape(groups, width, -1) for x in (mine, lax.ppermute(theirs, "col", inner))]

    def gather(at, to):
        slab = jnp.stack([x[:, at:to].reshape(groups * (to - at), -1) for x in payload])
        return lax.all_gather(slab, "row", axis=0)

    gathered = [gather(0, cut), gather(cut, width)]

    def send(now):
        return [lax.ppermute(now[0], "col", outer), lax.ppermute(now[1], "col", inner)]

    scale = 1.0 / HALF_WIDTH
    plans = [(scale, -CENTER * scale)] + [(2.0 * scale, -2.0 * CENTER * scale, -1.0)] * (2 * DEGREE - 2)
    plans.append((scale, -CENTER * scale, -0.5, 0.5))
    plans.append((1.0, 0.0))
    fields = [[part] for part in start]
    for at, plan in enumerate(plans):
        got = [send(fields[p][-1]) for p in range(PARTS)]
        for p in range(PARTS):
            now = fields[p][-1]
            used = [now] + (fields[p][-2:-1] if len(plan) > 2 else []) + ([start[p]] if len(plan) > 3 else [])
            (base,) = make_base(plan, weights, used, [])
            fields[p].append(make_tail(plan[0], base, got[p], weights, at == len(plans) - 1, []))
    filtered = [field[-2] for field in fields]
    image = [field[-1] for field in fields]
    other_filtered = [[lax.ppermute(filtered[p][0], "col", inner), got[p][1]] for p in range(PARTS)]
    other_image = [[lax.ppermute(image[p][0], "col", inner)] for p in range(PARTS)]

    everything = assemble(gathered[0], [])
    sums = reduce_step(product(everything, filtered, other_filtered), 1, True)
    image_sums = product(everything, image, other_image)
    *everything, sums, image_sums = assemble(gathered[1], [sums, image_sums])
    more = product(everything, filtered, other_filtered)
    more_image = product(everything, image, other_image)
    intersection = [reduce_rest(sums, 1, True), reduce_rest(more, 0, True)]
    projected_ham = [reduce_rest(image_sums, 0, False), reduce_rest(more_image, 0, False)]
    return jnp.concatenate(projected_ham, axis=0).T, jnp.concatenate(intersection, axis=0).T


def solution(mesh):
    in_specs = (P("row", "col", None), P("col", None, None, None), P("col", None))
    out_specs = (P("row", "col"), P("row", "col"))
    return jax.shard_map(
        per_device, mesh=mesh, in_specs=in_specs, out_specs=out_specs, check_vma=False
    )
```

```python
import functools

import jax
import jax.numpy as jnp
from jax import lax
from jax.experimental import pallas as pl
from jax.experimental.pallas import tpu as pltpu
from jax.sharding import PartitionSpec as P

REACH = 3
DEGREE = 3
CENTER = 0.5
HALF_WIDTH = 1.5
HSCALE = 0.1
PARTS = 2

WHOLE = pl.BlockSpec(memory_space=pltpu.VMEM)
SCALARS = pl.BlockSpec(memory_space=pltpu.SMEM)
ANYWHERE = pl.BlockSpec(memory_space=pl.ANY)
NN = ((1,), (0,))


def call(kernel, out_shape, arrays, specs, name, mib, flops=0, scratch=()):
    outs = out_shape if isinstance(out_shape, list) else [out_shape]
    moved = sum(a.size * a.dtype.itemsize for a in list(arrays) + outs)
    return pl.pallas_call(
        kernel,
        out_shape=out_shape,
        in_specs=specs,
        out_specs=[WHOLE] * len(outs) if isinstance(out_shape, list) else WHOLE,
        scratch_shapes=list(scratch),
        compiler_params=pltpu.CompilerParams(vmem_limit_bytes=mib * 1024 * 1024),
        cost_estimate=pl.CostEstimate(flops=int(flops), bytes_accessed=moved, transcendentals=0),
        name=name,
    )(*arrays)


def f32(*shape):
    return jax.ShapeDtypeStruct(shape, jnp.float32)


def bf16(*shape):
    return jax.ShapeDtypeStruct(shape, jnp.bfloat16)


def split(x):
    high = x.astype(jnp.bfloat16)
    low = (x - high.astype(jnp.float32)).astype(jnp.bfloat16)
    return high, low


def dot(a, b):
    return lax.dot_general(a, b, (NN, ((), ())), preferred_element_type=jnp.float32)


def dot3(a, b):
    rows = a[0].shape[0]
    both = dot(jnp.concatenate(a, axis=0), b[0])
    return both[:rows] + (both[rows:] + dot(a[0], b[1]))


def arrange_kernel(groups, width, odd_ref, v_ref, mine_ref, theirs_ref, *parts):
    odd = odd_ref[0]
    atoms, states, size = v_ref.shape
    half = atoms // 2
    rows = states // PARTS
    for k in range(atoms):
        column = v_ref[jnp.where(odd == 1, atoms - 1 - k, k)]
        at = slice((k % half) * size, (k % half + 1) * size)
        for part in range(PARTS):
            parts[2 * part + k // half][:, at] = column[part * rows : (part + 1) * rows]
        for group in range(groups):
            low = column[2 * group * width : (2 * group + 1) * width]
            high = column[(2 * group + 1) * width : (2 * group + 2) * width]
            to = slice(group * width, (group + 1) * width)
            mine_ref[to, k * size : (k + 1) * size] = jnp.where(odd == 1, high, low)
            theirs_ref[to, k * size : (k + 1) * size] = jnp.where(odd == 1, low, high)


def arrange(odd, vectors, width):
    states, atoms, size = vectors.shape
    out = [f32(states // 2, atoms * size)] * 2 + [f32(states // PARTS, atoms // 2 * size)] * (2 * PARTS)
    kernel = functools.partial(arrange_kernel, states // (2 * width), width)
    by_atom = jnp.transpose(vectors, (1, 0, 2))
    mine, theirs, *parts = call(kernel, out, [odd, by_atom], [SCALARS, WHOLE], "arrange", 16)
    return mine, theirs, [parts[2 * p : 2 * p + 2] for p in range(PARTS)]


def weights_kernel(atoms, odd_ref, coupling_ref, h_ref, own_h, own_l, far_h, far_l, near_h, near_l):
    odd = odd_ref[0]
    size = h_ref.shape[-1]

    def block(k, d):
        a = jnp.where(odd == 1, atoms - 1 - k, k)
        s = jnp.where(odd == 1, -d, d)
        h = HSCALE * h_ref[a, s + REACH]
        if d != 0:
            place = jnp.where(s < 0, s + REACH, s + REACH - 1)
            h = h * coupling_ref[a, place].astype(jnp.float32)
        return split(h.T)

    def put(high_ref, low_ref, row, column, value):
        rows = slice(row * size, (row + 1) * size)
        columns = slice(column * size, (column + 1) * size)
        high_ref[rows, columns], low_ref[rows, columns] = value

    zero = jnp.zeros((size, size), jnp.bfloat16)
    for m in range(atoms):
        for k in range(atoms):
            put(own_h, own_l, m, k, block(k, m - k) if abs(m - k) <= REACH else (zero, zero))
    for n in range(REACH):
        for j in range(REACH):
            d = -1 - n - j
            put(far_h, far_l, n, j, block(j, d) if d >= -REACH else (zero, zero))
            k = atoms - REACH + j
            d = atoms + REACH - 1 - n - k
            put(near_h, near_l, n, j, block(k, d) if d <= REACH else (zero, zero))


def make_weights(odd, coupling, hblocks):
    atoms, size = hblocks.shape[0], hblocks.shape[-1]
    full, edge = atoms * size, REACH * size
    out = [bf16(full, full)] * 2 + [bf16(edge, edge)] * 4
    kernel = functools.partial(weights_kernel, atoms)
    return call(kernel, out, [odd, coupling, hblocks], [SCALARS, SCALARS, WHOLE], "weights", 16)


def base_kernel(scales, high_ref, low_ref, *rest):
    out_ref = rest[-1]
    fields = [(rest[2 * i], rest[2 * i + 1]) for i in range((len(rest) - 1) // 2)]
    edge = rest[0].shape[1]
    halves = [split(ref[...]) for ref in fields[0]]
    operand = [jnp.concatenate([halves[0][term], halves[1][term]], axis=1) for term in range(2)]
    for side in range(2):
        columns = slice(side * edge, (side + 1) * edge)
        value = scales[0] * dot3(operand, (high_ref[:, columns], low_ref[:, columns]))
        for scale, field in zip(scales[1:], fields):
            if scale:
                value = value + scale * field[side][...]
        out_ref[:, columns] = value


def make_base(scales, weights, fields):
    arrays = list(weights[:2]) + [half for field in fields for half in field]
    rows, edge = fields[0][0].shape
    flops = 6 * rows * 4 * edge * edge
    return call(functools.partial(base_kernel, scales), f32(rows, 2 * edge), arrays, [WHOLE] * len(arrays), "base", 12, flops)


def tail_kernel(scale, base, got_far, got_near, fh, fl, nh, nl, *outs):
    edge = got_far.shape[1]
    for side, (got, high, low) in enumerate(((got_far, fh, fl), (got_near, nh, nl))):
        columns = slice(side * edge, (side + 1) * edge)
        value = base[:, columns] + scale * dot3(split(got[...]), (high[...], low[...]))
        if len(outs) == 2:
            outs[side][...] = value
        else:
            outs[0][:, columns] = value


def make_tail(scale, base, got, weights, joined):
    arrays = [base, *got, *weights[2:]]
    rows, edge = got[0].shape
    out = [f32(rows, 2 * edge)] if joined else [f32(rows, edge)] * 2
    flops = 6 * rows * 2 * edge * edge
    return call(functools.partial(tail_kernel, scale), out, arrays, [WHOLE] * len(arrays), "tail", 12, flops)


def assemble_kernel(count, place_ref, *refs):
    shards = refs[: 2 * count - 1]
    outs = refs[2 * count - 1 : -2]
    held, sems = refs[-2:]
    place = place_ref[0]
    rows, depth = shards[0].shape
    half = rows // 2

    def copies(plane, source):
        return [
            pltpu.make_async_copy(
                source.at[pl.ds(side * half, half)],
                held.at[pl.ds(plane * half, half), pl.ds(side * depth, depth)],
                sems.at[plane, side],
            )
            for side in range(2)
        ]

    for plane in range(count):
        for at in range(count):

            @pl.when(place == at)
            def _():
                for copy in copies(plane, shards[plane - at + count - 1]):
                    copy.start()

    for plane in range(count):
        for copy in copies(plane, shards[0]):
            copy.wait()
    step = 128
    for at in range(0, depth, step):
        for side in range(2):
            term = split(held[:, side * depth + at : side * depth + at + step].T)
            outs[2 * side][at : at + step], outs[2 * side + 1][at : at + step] = term


def assemble(place, shards):
    count = (len(shards) + 1) // 2
    rows, depth = shards[0].shape
    out = [bf16(depth, count * rows // 2)] * 4
    scratch = [pltpu.VMEM((count * rows // 2, 2 * depth), jnp.float32), pltpu.SemaphoreType.DMA((count, 2))]
    specs = [SCALARS] + [ANYWHERE] * len(shards)
    return call(functools.partial(assemble_kernel, count), out, [place] + shards, specs, "assemble", 24, 0, scratch)


def along_line(payload):
    count = lax.axis_size("row")
    before, after = [payload], [payload]
    for d in range(1, count):
        up = [(i, i + 1) for i in range(d - 1, count - 1)]
        down = [(count - 1 - a, count - 1 - b) for a, b in up]
        before.append(lax.ppermute(before[-1], "row", up))
        after.append(lax.ppermute(after[-1], "row", down))
    return before[:0:-1] + after


def tiles(width):
    step = 256 if width % 256 == 0 else width
    return width // step, step


def first_product_kernel(high_ref, low_ref, *rest):
    out_ref = rest[-1]
    operand = split(joined(rest[:-1]))
    count, step = tiles(out_ref.shape[1])

    @pl.loop(0, count)
    def _(i):
        columns = pl.ds(pl.multiple_of(i * step, step), step)
        out_ref[:, columns] = dot3(operand, (high_ref[:, columns], low_ref[:, columns]))


def second_product_kernel(high_ref, low_ref, acc_ref, *rest):
    out_ref = rest[-1]
    operand = split(joined(rest[:-1]))
    count, step = tiles(out_ref.shape[0])

    @pl.loop(0, count)
    def _(i):
        columns = pl.ds(pl.multiple_of(i * step, step), step)
        value = acc_ref[:, columns] + dot3(operand, (high_ref[:, columns], low_ref[:, columns]))
        out_ref[columns, :] = value.T


def joined(refs):
    parts = len(refs) // PARTS
    rows = [
        jnp.concatenate([ref[...] for ref in refs[parts * p : parts * (p + 1)]], axis=1) for p in range(PARTS)
    ]
    return jnp.concatenate(rows, axis=0)


def product(everything, own, other):
    depth, width = everything[0].shape
    rows = sum(part[0].shape[0] for part in own)
    flops = 6 * rows * depth * width
    mib = 24
    arrays = [half for part in own for half in part]
    arrays = [*everything[:2]] + [half for part in own for half in part]
    acc = call(first_product_kernel, f32(rows, width), arrays, [WHOLE] * len(arrays), "own_product", mib, flops)
    arrays = [*everything[2:], acc] + [half for part in other for half in part]
    return call(second_product_kernel, f32(width, rows), arrays, [WHOLE] * len(arrays), "other_product", mib, flops)


def halve(part, axis_at, mine, count, bit):
    other = lax.dynamic_index_in_dim(part, 1 - mine, axis_at, keepdims=False)
    kept = lax.dynamic_index_in_dim(part, mine, axis_at, keepdims=False)
    return kept + lax.ppermute(other, "col", [(i, i ^ (1 << bit)) for i in range(count)])


def reduce_chips(part):
    count = lax.axis_size("col")
    me = lax.axis_index("col").astype(jnp.int32)
    bits = count.bit_length() - 1
    width = part.shape[0] * 2 // count
    part = part.reshape((2,) * (bits - 1) + (width, part.shape[1]))
    cut = width // 2
    first, second = part[..., :cut, :], part[..., cut:, :]
    for step in range(1, bits):
        low, high = step, bits - step
        first = halve(first, bits - 1 - step, (me >> low) % 2, count, low)
        second = halve(second, 0, (me >> high) % 2, count, high)
    return jnp.concatenate([first, second], axis=0).T


def per_device(vectors, hblocks, coupling):
    count = lax.axis_size("col")
    me = lax.axis_index("col").astype(jnp.int32)
    place = lax.axis_index("row").astype(jnp.int32).reshape(1)
    odd = (me % 2).reshape(1)
    width = vectors.shape[0] * lax.axis_size("row") // count
    inner = [(i, i ^ 1) for i in range(count)]
    outer = [(i, i + 1) for i in range(1, count - 1, 2)]
    outer = outer + [(b, a) for a, b in outer]

    mine, theirs, start = arrange(odd, vectors, width)
    weights = make_weights(odd, coupling, hblocks)
    everything = assemble(
        place, along_line(jnp.concatenate([mine, lax.ppermute(theirs, "col", inner)], axis=0))
    )

    def send(now):
        return [lax.ppermute(now[0], "col", outer), lax.ppermute(now[1], "col", inner)]

    scale = 1.0 / HALF_WIDTH
    plans = [(scale, -CENTER * scale)] + [(2.0 * scale, -2.0 * CENTER * scale, -1.0)] * (2 * DEGREE - 2)
    plans.append((scale, -CENTER * scale, -0.5, 0.5))
    plans.append((1.0, 0.0))
    fields = [[part] for part in start]
    for at, plan in enumerate(plans):
        last = at == len(plans) - 1
        got = []
        for p in range(PARTS):
            now = fields[p][-1]
            got.append(send(now))
            used = [now] + (fields[p][-2:-1] if len(plan) > 2 else []) + ([start[p]] if len(plan) > 3 else [])
            base = make_base(plan, weights, used)
            fields[p].append(make_tail(plan[0], base, got[p], weights, last))
    filtered = [field[-2] for field in fields]
    image = [field[-1] for field in fields]
    other = [[lax.ppermute(filtered[p][0], "col", inner), got[p][1]] for p in range(PARTS)]
    intersection = reduce_chips(product(everything, filtered, other))
    other = [[lax.ppermute(image[p][0], "col", inner)] for p in range(PARTS)]
    projected_ham = reduce_chips(product(everything, image, other))
    return projected_ham, intersection


def solution(mesh):
    in_specs = (P("row", "col", None), P("col", None, None, None), P("col", None))
    out_specs = (P("row", "col"), P("row", "col"))
    return jax.shard_map(
        per_device, mesh=mesh, in_specs=in_specs, out_specs=out_specs, check_vma=False
    )
```

```python
import functools

import jax
import jax.numpy as jnp
from jax import lax
from jax.experimental import pallas as pl
from jax.experimental.pallas import tpu as pltpu
from jax.sharding import PartitionSpec as P

REACH = 3
DEGREE = 3
CENTER = 0.5
HALF_WIDTH = 1.5
HSCALE = 0.1
PARTS = 2

WHOLE = pl.BlockSpec(memory_space=pltpu.VMEM)
SCALARS = pl.BlockSpec(memory_space=pltpu.SMEM)
ANYWHERE = pl.BlockSpec(memory_space=pl.ANY)
NN = ((1,), (0,))


def call(kernel, out_shape, arrays, specs, name, mib, flops=0, scratch=()):
    outs = out_shape if isinstance(out_shape, list) else [out_shape]
    moved = sum(a.size * a.dtype.itemsize for a in list(arrays) + outs)
    return pl.pallas_call(
        kernel,
        out_shape=out_shape,
        in_specs=specs,
        out_specs=[WHOLE] * len(outs) if isinstance(out_shape, list) else WHOLE,
        scratch_shapes=list(scratch),
        compiler_params=pltpu.CompilerParams(vmem_limit_bytes=mib * 1024 * 1024),
        cost_estimate=pl.CostEstimate(flops=int(flops), bytes_accessed=moved, transcendentals=0),
        name=name,
    )(*arrays)


def f32(*shape):
    return jax.ShapeDtypeStruct(shape, jnp.float32)


def bf16(*shape):
    return jax.ShapeDtypeStruct(shape, jnp.bfloat16)


def split(x):
    high = x.astype(jnp.bfloat16)
    low = (x - high.astype(jnp.float32)).astype(jnp.bfloat16)
    return high, low


def dot(a, b):
    return lax.dot_general(a, b, (NN, ((), ())), preferred_element_type=jnp.float32)


def dot3(a, b):
    rows = a[0].shape[0]
    both = dot(jnp.concatenate(a, axis=0), b[0])
    return both[:rows] + (both[rows:] + dot(a[0], b[1]))


def arrange_kernel(groups, width, odd_ref, v_ref, mine_ref, theirs_ref, *parts):
    odd = odd_ref[0]
    atoms, states, size = v_ref.shape
    half = atoms // 2
    rows = states // PARTS
    for k in range(atoms):
        column = v_ref[jnp.where(odd == 1, atoms - 1 - k, k)]
        at = slice((k % half) * size, (k % half + 1) * size)
        for part in range(PARTS):
            parts[2 * part + k // half][:, at] = column[part * rows : (part + 1) * rows]
        for group in range(groups):
            low = column[2 * group * width : (2 * group + 1) * width]
            high = column[(2 * group + 1) * width : (2 * group + 2) * width]
            to = slice(group * width, (group + 1) * width)
            mine_ref[to, k * size : (k + 1) * size] = jnp.where(odd == 1, high, low)
            theirs_ref[to, k * size : (k + 1) * size] = jnp.where(odd == 1, low, high)


def arrange(odd, vectors, width):
    states, atoms, size = vectors.shape
    out = [f32(states // 2, atoms * size)] * 2 + [f32(states // PARTS, atoms // 2 * size)] * (2 * PARTS)
    kernel = functools.partial(arrange_kernel, states // (2 * width), width)
    by_atom = jnp.transpose(vectors, (1, 0, 2))
    mine, theirs, *parts = call(kernel, out, [odd, by_atom], [SCALARS, WHOLE], "arrange", 16)
    return mine, theirs, [parts[2 * p : 2 * p + 2] for p in range(PARTS)]


def weights_kernel(atoms, odd_ref, coupling_ref, h_ref, own_h, own_l, far_h, far_l, near_h, near_l):
    odd = odd_ref[0]
    size = h_ref.shape[-1]

    def block(k, d):
        a = jnp.where(odd == 1, atoms - 1 - k, k)
        s = jnp.where(odd == 1, -d, d)
        h = HSCALE * h_ref[a, s + REACH]
        if d != 0:
            place = jnp.where(s < 0, s + REACH, s + REACH - 1)
            h = h * coupling_ref[a, place].astype(jnp.float32)
        return split(h.T)

    def put(high_ref, low_ref, row, column, value):
        rows = slice(row * size, (row + 1) * size)
        columns = slice(column * size, (column + 1) * size)
        high_ref[rows, columns], low_ref[rows, columns] = value

    zero = jnp.zeros((size, size), jnp.bfloat16)
    for m in range(atoms):
        for k in range(atoms):
            put(own_h, own_l, m, k, block(k, m - k) if abs(m - k) <= REACH else (zero, zero))
    for n in range(REACH):
        for j in range(REACH):
            d = -1 - n - j
            put(far_h, far_l, n, j, block(j, d) if d >= -REACH else (zero, zero))
            k = atoms - REACH + j
            d = atoms + REACH - 1 - n - k
            put(near_h, near_l, n, j, block(k, d) if d <= REACH else (zero, zero))


def make_weights(odd, coupling, hblocks):
    atoms, size = hblocks.shape[0], hblocks.shape[-1]
    full, edge = atoms * size, REACH * size
    out = [bf16(full, full)] * 2 + [bf16(edge, edge)] * 4
    kernel = functools.partial(weights_kernel, atoms)
    return call(kernel, out, [odd, coupling, hblocks], [SCALARS, SCALARS, WHOLE], "weights", 16)


def base_kernel(scales, high_ref, low_ref, *rest):
    out_ref = rest[-1]
    fields = [(rest[2 * i], rest[2 * i + 1]) for i in range((len(rest) - 1) // 2)]
    edge = rest[0].shape[1]
    halves = [split(ref[...]) for ref in fields[0]]
    operand = [jnp.concatenate([halves[0][term], halves[1][term]], axis=1) for term in range(2)]
    for side in range(2):
        columns = slice(side * edge, (side + 1) * edge)
        value = scales[0] * dot3(operand, (high_ref[:, columns], low_ref[:, columns]))
        for scale, field in zip(scales[1:], fields):
            if scale:
                value = value + scale * field[side][...]
        out_ref[:, columns] = value


def make_base(scales, weights, fields):
    arrays = list(weights[:2]) + [half for field in fields for half in field]
    rows, edge = fields[0][0].shape
    flops = 6 * rows * 4 * edge * edge
    return call(functools.partial(base_kernel, scales), f32(rows, 2 * edge), arrays, [WHOLE] * len(arrays), "base", 12, flops)


def tail_kernel(scale, base, got_far, got_near, fh, fl, nh, nl, *outs):
    edge = got_far.shape[1]
    for side, (got, high, low) in enumerate(((got_far, fh, fl), (got_near, nh, nl))):
        columns = slice(side * edge, (side + 1) * edge)
        value = base[:, columns] + scale * dot3(split(got[...]), (high[...], low[...]))
        if len(outs) == 2:
            outs[side][...] = value
        else:
            outs[0][:, columns] = value


def make_tail(scale, base, got, weights, joined):
    arrays = [base, *got, *weights[2:]]
    rows, edge = got[0].shape
    out = [f32(rows, 2 * edge)] if joined else [f32(rows, edge)] * 2
    flops = 6 * rows * 2 * edge * edge
    return call(functools.partial(tail_kernel, scale), out, arrays, [WHOLE] * len(arrays), "tail", 12, flops)


def assemble_kernel(count, place_ref, *refs):
    shards = refs[: 2 * count - 1]
    outs = refs[2 * count - 1 : -2]
    held, sems = refs[-2:]
    place = place_ref[0]
    rows, depth = shards[0].shape
    half = rows // 2

    def copies(plane, source):
        return [
            pltpu.make_async_copy(
                source.at[pl.ds(side * half, half)],
                held.at[pl.ds(plane * half, half), pl.ds(side * depth, depth)],
                sems.at[plane, side],
            )
            for side in range(2)
        ]

    for plane in range(count):
        for at in range(count):

            @pl.when(place == at)
            def _():
                for copy in copies(plane, shards[plane - at + count - 1]):
                    copy.start()

    for plane in range(count):
        for copy in copies(plane, shards[0]):
            copy.wait()
    step = 128
    for at in range(0, depth, step):
        for side in range(2):
            term = split(held[:, side * depth + at : side * depth + at + step].T)
            outs[2 * side][at : at + step], outs[2 * side + 1][at : at + step] = term


def assemble(place, shards):
    count = (len(shards) + 1) // 2
    rows, depth = shards[0].shape
    out = [bf16(depth, count * rows // 2)] * 4
    scratch = [pltpu.VMEM((count * rows // 2, 2 * depth), jnp.float32), pltpu.SemaphoreType.DMA((count, 2))]
    specs = [SCALARS] + [ANYWHERE] * len(shards)
    return call(functools.partial(assemble_kernel, count), out, [place] + shards, specs, "assemble", 24, 0, scratch)


def along_line(payload):
    count = lax.axis_size("row")
    before, after = [payload], [payload]
    for d in range(1, count):
        up = [(i, i + 1) for i in range(d - 1, count - 1)]
        down = [(count - 1 - a, count - 1 - b) for a, b in up]
        before.append(lax.ppermute(before[-1], "row", up))
        after.append(lax.ppermute(after[-1], "row", down))
    return before[:0:-1] + after


def first_product_kernel(high_ref, low_ref, *rest):
    out_ref = rest[-1]
    out_ref[...] = dot3(split(joined(rest[:-1])), (high_ref[...], low_ref[...]))


def second_product_kernel(high_ref, low_ref, acc_ref, *rest):
    out_ref = rest[-1]
    value = acc_ref[...] + dot3(split(joined(rest[:-1])), (high_ref[...], low_ref[...]))
    out_ref[...] = value.T


def joined(refs):
    parts = len(refs) // PARTS
    rows = [
        jnp.concatenate([ref[...] for ref in refs[parts * p : parts * (p + 1)]], axis=1) for p in range(PARTS)
    ]
    return jnp.concatenate(rows, axis=0)


def product(everything, own, other):
    depth, width = everything[0].shape
    rows = sum(part[0].shape[0] for part in own)
    flops = 6 * rows * depth * width
    mib = 24
    arrays = [half for part in own for half in part]
    arrays = [*everything[:2]] + [half for part in own for half in part]
    acc = call(first_product_kernel, f32(rows, width), arrays, [WHOLE] * len(arrays), "own_product", mib, flops)
    arrays = [*everything[2:], acc] + [half for part in other for half in part]
    return call(second_product_kernel, f32(width, rows), arrays, [WHOLE] * len(arrays), "other_product", mib, flops)


def halve(part, axis_at, mine, count, bit):
    other = lax.dynamic_index_in_dim(part, 1 - mine, axis_at, keepdims=False)
    kept = lax.dynamic_index_in_dim(part, mine, axis_at, keepdims=False)
    return kept + lax.ppermute(other, "col", [(i, i ^ (1 << bit)) for i in range(count)])


def reduce_chips(part):
    count = lax.axis_size("col")
    me = lax.axis_index("col").astype(jnp.int32)
    bits = count.bit_length() - 1
    width = part.shape[0] * 2 // count
    part = part.reshape((2,) * (bits - 1) + (width, part.shape[1]))
    cut = width // 2
    first, second = part[..., :cut, :], part[..., cut:, :]
    for step in range(1, bits):
        low, high = step, bits - step
        first = halve(first, bits - 1 - step, (me >> low) % 2, count, low)
        second = halve(second, 0, (me >> high) % 2, count, high)
    return jnp.concatenate([first, second], axis=0).T


def per_device(vectors, hblocks, coupling):
    count = lax.axis_size("col")
    me = lax.axis_index("col").astype(jnp.int32)
    place = lax.axis_index("row").astype(jnp.int32).reshape(1)
    odd = (me % 2).reshape(1)
    width = vectors.shape[0] * lax.axis_size("row") // count
    inner = [(i, i ^ 1) for i in range(count)]
    outer = [(i, i + 1) for i in range(1, count - 1, 2)]
    outer = outer + [(b, a) for a, b in outer]

    mine, theirs, start = arrange(odd, vectors, width)
    weights = make_weights(odd, coupling, hblocks)
    everything = assemble(
        place, along_line(jnp.concatenate([mine, lax.ppermute(theirs, "col", inner)], axis=0))
    )

    def send(now):
        return [lax.ppermute(now[0], "col", outer), lax.ppermute(now[1], "col", inner)]

    scale = 1.0 / HALF_WIDTH
    plans = [(scale, -CENTER * scale)] + [(2.0 * scale, -2.0 * CENTER * scale, -1.0)] * (2 * DEGREE - 2)
    plans.append((scale, -CENTER * scale, -0.5, 0.5))
    plans.append((1.0, 0.0))
    fields = [[part] for part in start]
    for at, plan in enumerate(plans):
        last = at == len(plans) - 1
        got = []
        for p in range(PARTS):
            now = fields[p][-1]
            got.append(send(now))
            used = [now] + (fields[p][-2:-1] if len(plan) > 2 else []) + ([start[p]] if len(plan) > 3 else [])
            base = make_base(plan, weights, used)
            fields[p].append(make_tail(plan[0], base, got[p], weights, last))
    filtered = [field[-2] for field in fields]
    image = [field[-1] for field in fields]
    other = [[lax.ppermute(filtered[p][0], "col", inner), got[p][1]] for p in range(PARTS)]
    intersection = reduce_chips(product(everything, filtered, other))
    other = [[lax.ppermute(image[p][0], "col", inner)] for p in range(PARTS)]
    projected_ham = reduce_chips(product(everything, image, other))
    return projected_ham, intersection


def solution(mesh):
    in_specs = (P("row", "col", None), P("col", None, None, None), P("col", None))
    out_specs = (P("row", "col"), P("row", "col"))
    return jax.shard_map(
        per_device, mesh=mesh, in_specs=in_specs, out_specs=out_specs, check_vma=False
    )
```

```python
import functools

import jax
import jax.numpy as jnp
from jax import lax
from jax.experimental import pallas as pl
from jax.experimental.pallas import tpu as pltpu
from jax.sharding import PartitionSpec as P

REACH = 3
DEGREE = 3
CENTER = 0.5
HALF_WIDTH = 1.5
HSCALE = 0.1
PARTS = 2

WHOLE = pl.BlockSpec(memory_space=pltpu.VMEM)
SCALARS = pl.BlockSpec(memory_space=pltpu.SMEM)
ANYWHERE = pl.BlockSpec(memory_space=pl.ANY)
NN = ((1,), (0,))


def call(kernel, out_shape, arrays, specs, name, mib, flops=0, scratch=()):
    outs = out_shape if isinstance(out_shape, list) else [out_shape]
    moved = sum(a.size * a.dtype.itemsize for a in list(arrays) + outs)
    return pl.pallas_call(
        kernel,
        out_shape=out_shape,
        in_specs=specs,
        out_specs=[WHOLE] * len(outs) if isinstance(out_shape, list) else WHOLE,
        scratch_shapes=list(scratch),
        compiler_params=pltpu.CompilerParams(vmem_limit_bytes=mib * 1024 * 1024),
        cost_estimate=pl.CostEstimate(flops=int(flops), bytes_accessed=moved, transcendentals=0),
        name=name,
    )(*arrays)


def f32(*shape):
    return jax.ShapeDtypeStruct(shape, jnp.float32)


def bf16(*shape):
    return jax.ShapeDtypeStruct(shape, jnp.bfloat16)


def split(x):
    high = x.astype(jnp.bfloat16)
    low = (x - high.astype(jnp.float32)).astype(jnp.bfloat16)
    return high, low


def dot(a, b):
    return lax.dot_general(a, b, (NN, ((), ())), preferred_element_type=jnp.float32)


def dot3(a, b):
    rows = a[0].shape[0]
    both = dot(jnp.concatenate(a, axis=0), b[0])
    return both[:rows] + (both[rows:] + dot(a[0], b[1]))


def arrange_kernel(groups, width, odd_ref, v_ref, mine_ref, theirs_ref, *parts):
    odd = odd_ref[0]
    atoms, states, size = v_ref.shape
    half = atoms // 2
    rows = states // PARTS
    for k in range(atoms):
        column = v_ref[jnp.where(odd == 1, atoms - 1 - k, k)]
        at = slice((k % half) * size, (k % half + 1) * size)
        for part in range(PARTS):
            parts[2 * part + k // half][:, at] = column[part * rows : (part + 1) * rows]
        for group in range(groups):
            low = column[2 * group * width : (2 * group + 1) * width]
            high = column[(2 * group + 1) * width : (2 * group + 2) * width]
            to = slice(group * width, (group + 1) * width)
            mine_ref[to, k * size : (k + 1) * size] = jnp.where(odd == 1, high, low)
            theirs_ref[to, k * size : (k + 1) * size] = jnp.where(odd == 1, low, high)


def arrange(odd, vectors, width):
    states, atoms, size = vectors.shape
    out = [f32(states // 2, atoms * size)] * 2 + [f32(states // PARTS, atoms // 2 * size)] * (2 * PARTS)
    kernel = functools.partial(arrange_kernel, states // (2 * width), width)
    by_atom = jnp.transpose(vectors, (1, 0, 2))
    mine, theirs, *parts = call(kernel, out, [odd, by_atom], [SCALARS, WHOLE], "arrange", 16)
    return mine, theirs, [parts[2 * p : 2 * p + 2] for p in range(PARTS)]


def weights_kernel(atoms, odd_ref, coupling_ref, h_ref, own_h, own_l, far_h, far_l, near_h, near_l):
    odd = odd_ref[0]
    size = h_ref.shape[-1]

    def block(k, d):
        a = jnp.where(odd == 1, atoms - 1 - k, k)
        s = jnp.where(odd == 1, -d, d)
        h = HSCALE * h_ref[a, s + REACH]
        if d != 0:
            place = jnp.where(s < 0, s + REACH, s + REACH - 1)
            h = h * coupling_ref[a, place].astype(jnp.float32)
        return split(h.T)

    def put(high_ref, low_ref, row, column, value):
        rows = slice(row * size, (row + 1) * size)
        columns = slice(column * size, (column + 1) * size)
        high_ref[rows, columns], low_ref[rows, columns] = value

    zero = jnp.zeros((size, size), jnp.bfloat16)
    for m in range(atoms):
        for k in range(atoms):
            put(own_h, own_l, m, k, block(k, m - k) if abs(m - k) <= REACH else (zero, zero))
    for n in range(REACH):
        for j in range(REACH):
            d = -1 - n - j
            put(far_h, far_l, n, j, block(j, d) if d >= -REACH else (zero, zero))
            k = atoms - REACH + j
            d = atoms + REACH - 1 - n - k
            put(near_h, near_l, n, j, block(k, d) if d <= REACH else (zero, zero))


def make_weights(odd, coupling, hblocks):
    atoms, size = hblocks.shape[0], hblocks.shape[-1]
    full, edge = atoms * size, REACH * size
    out = [bf16(full, full)] * 2 + [bf16(edge, edge)] * 4
    kernel = functools.partial(weights_kernel, atoms)
    return call(kernel, out, [odd, coupling, hblocks], [SCALARS, SCALARS, WHOLE], "weights", 16)


def base_kernel(scales, high_ref, low_ref, *rest):
    out_ref = rest[-1]
    fields = [(rest[2 * i], rest[2 * i + 1]) for i in range((len(rest) - 1) // 2)]
    edge = rest[0].shape[1]
    halves = [split(ref[...]) for ref in fields[0]]
    operand = [jnp.concatenate([halves[0][term], halves[1][term]], axis=1) for term in range(2)]
    for side in range(2):
        columns = slice(side * edge, (side + 1) * edge)
        value = scales[0] * dot3(operand, (high_ref[:, columns], low_ref[:, columns]))
        for scale, field in zip(scales[1:], fields):
            if scale:
                value = value + scale * field[side][...]
        out_ref[:, columns] = value


def make_base(scales, weights, fields):
    arrays = list(weights[:2]) + [half for field in fields for half in field]
    rows, edge = fields[0][0].shape
    flops = 6 * rows * 4 * edge * edge
    return call(functools.partial(base_kernel, scales), f32(rows, 2 * edge), arrays, [WHOLE] * len(arrays), "base", 12, flops)


def tail_kernel(scale, base, got_far, got_near, fh, fl, nh, nl, *outs):
    edge = got_far.shape[1]
    for side, (got, high, low) in enumerate(((got_far, fh, fl), (got_near, nh, nl))):
        columns = slice(side * edge, (side + 1) * edge)
        value = base[:, columns] + scale * dot3(split(got[...]), (high[...], low[...]))
        if len(outs) == 2:
            outs[side][...] = value
        else:
            outs[0][:, columns] = value


def make_tail(scale, base, got, weights, joined):
    arrays = [base, *got, *weights[2:]]
    rows, edge = got[0].shape
    out = [f32(rows, 2 * edge)] if joined else [f32(rows, edge)] * 2
    flops = 6 * rows * 2 * edge * edge
    return call(functools.partial(tail_kernel, scale), out, arrays, [WHOLE] * len(arrays), "tail", 12, flops)


def assemble_kernel(count, place_ref, *refs):
    shards = refs[: 2 * count - 3]
    outs = refs[2 * count - 3 : -2]
    held, sems = refs[-2:]
    place = place_ref[0]
    rows, depth = shards[0].shape
    half = rows // 2

    def copies(plane, source):
        return [
            pltpu.make_async_copy(
                source.at[pl.ds(side * half, half)],
                held.at[pl.ds(plane * half, half), pl.ds(side * depth, depth)],
                sems.at[plane, side],
            )
            for side in range(2)
        ]

    for at in range(count):

        @pl.when(place == at)
        def _():
            for plane in range(count):
                if abs(plane - at) < count - 1:
                    for copy in copies(plane, shards[plane - at + count - 2]):
                        copy.start()
                else:
                    held[plane * half : (plane + 1) * half] = jnp.zeros((half, 2 * depth), jnp.float32)
            for plane in range(count):
                if abs(plane - at) < count - 1:
                    for copy in copies(plane, shards[plane - at + count - 2]):
                        copy.wait()

    step = 128
    for at in range(0, depth, step):
        for side in range(2):
            term = split(held[:, side * depth + at : side * depth + at + step].T)
            outs[2 * side][at : at + step], outs[2 * side + 1][at : at + step] = term


def assemble(place, before, after):
    count = len(before)
    shards = before[count - 2 : 0 : -1] + after[: count - 1]
    rows, depth = shards[0].shape
    out = [bf16(depth, count * rows // 2)] * 4
    scratch = [pltpu.VMEM((count * rows // 2, 2 * depth), jnp.float32), pltpu.SemaphoreType.DMA((count, 2))]
    specs = [SCALARS] + [ANYWHERE] * len(shards)
    return call(functools.partial(assemble_kernel, count), out, [place] + shards, specs, "assemble", 24, 0, scratch)


def late_kernel(before_ref, after_ref, *outs):
    rows, depth = before_ref.shape
    half = rows // 2
    step = 128
    for side in range(2):
        here = slice(side * half, (side + 1) * half)
        for at in range(0, depth, step):
            columns = slice(at, at + step)
            term = split((before_ref[here, columns] + after_ref[here, columns]).T)
            outs[2 * side][columns], outs[2 * side + 1][columns] = term


def assemble_late(before, after):
    rows, depth = before[-1].shape
    out = [bf16(depth, rows // 2)] * 4
    return call(late_kernel, out, [before[-1], after[-1]], [WHOLE] * 2, "late", 16)


def finish_kernel(count, place_ref, early_ref, own_h, own_l, other_h, other_l, *rest):
    out_ref = rest[-1]
    place = place_ref[0]
    half = len(rest) // 2
    value = dot3(split(joined(rest[:half])), (own_h[...], own_l[...]))
    value = (value + dot3(split(joined(rest[half:-1])), (other_h[...], other_l[...]))).T
    width = value.shape[0]
    out_ref[...] = early_ref[...]

    @pl.when(place == 0)
    def _():
        out_ref[(count - 1) * width :] = value

    @pl.when(place == count - 1)
    def _():
        out_ref[:width] = value


def finish(place, early, late, own, other):
    depth, width = late[0].shape
    count = early.shape[0] // width
    arrays = [place, early, *late] + [half for part in own + other for half in part]
    specs = [SCALARS] + [WHOLE] * (len(arrays) - 1)
    flops = 12 * early.shape[1] * depth * width
    return call(functools.partial(finish_kernel, count), f32(*early.shape), arrays, specs, "finish", 24, flops)


def along_line(payload):
    count = lax.axis_size("row")
    before, after = [payload], [payload]
    for d in range(1, count):
        up = [(i, i + 1) for i in range(d - 1, count - 1)]
        down = [(count - 1 - a, count - 1 - b) for a, b in up]
        before.append(lax.ppermute(before[-1], "row", up))
        after.append(lax.ppermute(after[-1], "row", down))
    return before, after


def first_product_kernel(high_ref, low_ref, *rest):
    out_ref = rest[-1]
    out_ref[...] = dot3(split(joined(rest[:-1])), (high_ref[...], low_ref[...]))


def second_product_kernel(high_ref, low_ref, acc_ref, *rest):
    out_ref = rest[-1]
    value = acc_ref[...] + dot3(split(joined(rest[:-1])), (high_ref[...], low_ref[...]))
    out_ref[...] = value.T


def joined(refs):
    parts = len(refs) // PARTS
    rows = [
        jnp.concatenate([ref[...] for ref in refs[parts * p : parts * (p + 1)]], axis=1) for p in range(PARTS)
    ]
    return jnp.concatenate(rows, axis=0)


def product(everything, own, other):
    depth, width = everything[0].shape
    rows = sum(part[0].shape[0] for part in own)
    flops = 6 * rows * depth * width
    mib = 24
    arrays = [half for part in own for half in part]
    arrays = [*everything[:2]] + [half for part in own for half in part]
    acc = call(first_product_kernel, f32(rows, width), arrays, [WHOLE] * len(arrays), "own_product", mib, flops)
    arrays = [*everything[2:], acc] + [half for part in other for half in part]
    return call(second_product_kernel, f32(width, rows), arrays, [WHOLE] * len(arrays), "other_product", mib, flops)


def halve(part, axis_at, mine, count, bit):
    other = lax.dynamic_index_in_dim(part, 1 - mine, axis_at, keepdims=False)
    kept = lax.dynamic_index_in_dim(part, mine, axis_at, keepdims=False)
    return kept + lax.ppermute(other, "col", [(i, i ^ (1 << bit)) for i in range(count)])


def reduce_chips(part):
    count = lax.axis_size("col")
    me = lax.axis_index("col").astype(jnp.int32)
    bits = count.bit_length() - 1
    width = part.shape[0] * 2 // count
    part = part.reshape((2,) * (bits - 1) + (width, part.shape[1]))
    cut = width // 2
    first, second = part[..., :cut, :], part[..., cut:, :]
    for step in range(1, bits):
        low, high = step, bits - step
        first = halve(first, bits - 1 - step, (me >> low) % 2, count, low)
        second = halve(second, 0, (me >> high) % 2, count, high)
    return jnp.concatenate([first, second], axis=0).T


def per_device(vectors, hblocks, coupling):
    count = lax.axis_size("col")
    me = lax.axis_index("col").astype(jnp.int32)
    place = lax.axis_index("row").astype(jnp.int32).reshape(1)
    odd = (me % 2).reshape(1)
    width = vectors.shape[0] * lax.axis_size("row") // count
    inner = [(i, i ^ 1) for i in range(count)]
    outer = [(i, i + 1) for i in range(1, count - 1, 2)]
    outer = outer + [(b, a) for a, b in outer]

    mine, theirs, start = arrange(odd, vectors, width)
    weights = make_weights(odd, coupling, hblocks)
    before, after = along_line(jnp.concatenate([mine, lax.ppermute(theirs, "col", inner)], axis=0))
    everything = assemble(place, before, after)
    late = assemble_late(before, after)

    def send(now):
        return [lax.ppermute(now[0], "col", outer), lax.ppermute(now[1], "col", inner)]

    scale = 1.0 / HALF_WIDTH
    plans = [(scale, -CENTER * scale)] + [(2.0 * scale, -2.0 * CENTER * scale, -1.0)] * (2 * DEGREE - 2)
    plans.append((scale, -CENTER * scale, -0.5, 0.5))
    plans.append((1.0, 0.0))
    fields = [[part] for part in start]
    for at, plan in enumerate(plans):
        last = at == len(plans) - 1
        got = []
        for p in range(PARTS):
            now = fields[p][-1]
            got.append(send(now))
            used = [now] + (fields[p][-2:-1] if len(plan) > 2 else []) + ([start[p]] if len(plan) > 3 else [])
            base = make_base(plan, weights, used)
            fields[p].append(make_tail(plan[0], base, got[p], weights, last))
    filtered = [field[-2] for field in fields]
    image = [field[-1] for field in fields]
    other = [[lax.ppermute(filtered[p][0], "col", inner), got[p][1]] for p in range(PARTS)]
    sums = product(everything, filtered, other)
    other_image = [[lax.ppermute(image[p][0], "col", inner)] for p in range(PARTS)]
    image_sums = product(everything, image, other_image)
    intersection = reduce_chips(finish(place, sums, late, filtered, other))
    projected_ham = reduce_chips(finish(place, image_sums, late, image, other_image))
    return projected_ham, intersection


def solution(mesh):
    in_specs = (P("row", "col", None), P("col", None, None, None), P("col", None))
    out_specs = (P("row", "col"), P("row", "col"))
    return jax.shard_map(
        per_device, mesh=mesh, in_specs=in_specs, out_specs=out_specs, check_vma=False
    )
```
